512 devices in a mesh: tile: 128 (over x, z, core), band: 4 (over y).
Axes of the slice: x: 4, y: 4, z: 16, core: 2. Of those that a mesh axis runs over, the one named last changes fastest.
Arguments:
- column_state: bfloat16 [16384, 512], P('tile'), may hold values from -6 to 6
- sunlit: int32 [16384], P('tile'), may hold values from 0 to 1, as said below
- flagged: int32 [16384], P('tile'), may hold values from 0 to 1, as said below
- cos_zenith: bfloat16 [16384], P('tile'), may hold values from 0.05 to 1
- surface_albedo: bfloat16 [16384], P('tile'), may hold values from 0.29882812 to 0.8984375
- first_weight: bfloat16 [4, 512, 1024], P('band'), may hold values from -0.25 to 0.25
- first_bias: bfloat16 [4, 1024], P('band'), may hold values from -3 to 3
- second_weight: bfloat16 [4, 1024, 256], P('band'), may hold values from -0.1875 to 0.1875
- second_bias: bfloat16 [4, 256], P('band'), may hold values from -3 to 3
- absorption: float32 [224, 128], P('band'), may hold values from 0.00015625 to 0.15625
- scatter_albedo: float32 [224], P('band'), may hold values from 0.85 to 0.995
- solar_weight: float32 [224], P('band'), may hold values from 0.004464286 to 0.04464286
Outputs:
- fluxes: float32 [16384, 256], P(('tile', 'band'))
The draws below stay inside these ranges and needn't reach their ends.
Inputs may be any that keep to these rules, and one draw needn't show every extreme that they name: Exactly a quarter of the 16384 columns are flagged, and every one of the 128 columns of at least one tile is flagged. Every flagged column is sunlit.
All inputs are finite; a program needn't handle non-finite values.
Results may differ from the reference program's by a relative error of at most 0.0017.
The reference program's roundings to bfloat16 on the way count: a program that leaves them out, or rounds other values in their place, can miss the bound.
Values may be sent and summed in bfloat16 or wider, within the bound.
No kernel may reach another device: no remote copies, remote signals or barrier semaphores. Data moves between devices by JAX's collectives and lax.ppermute only.
A program may use at most 64 MiB of HBM per device.

```python
import math
import jax
import jax.numpy as jnp
from jax import lax

LEV = 128
HID = 1024
G = 224
SWEEPS = 4
COLS_T = 128
MEMBERS = 4
FEAT = 512
OUTW = 256
COLS = 16384
PER = 32
N_TILE = 128


def flag_pattern(key):
    key = jax.random.fold_in(key, 7)
    tile_key, noise_key = jax.random.split(key)
    tile_order = jax.random.permutation(tile_key, N_TILE)
    tile_of = jnp.arange(COLS) // COLS_T
    order_of = tile_order[tile_of]
    score_base = order_of * (COLS_T // 2) + jnp.where(order_of == N_TILE - 1, COLS, 0)
    noise = jax.random.randint(noise_key, (COLS,), 0, COLS_T)
    scores = (score_base + noise).astype(jnp.int32)
    picked = jnp.argsort(-scores, stable=True)[:COLS // 4]
    return jnp.zeros((COLS,), jnp.int32).at[picked].set(1)


def draw_flagged(key, part):
    return flag_pattern(key)


def draw_sunlit(key, part):
    flags = flag_pattern(key)
    key = jax.random.fold_in(key, 11)
    daylight = jax.random.randint(key, (COLS,), 0, 2).astype(jnp.int32)
    return jnp.maximum(flags, daylight).astype(jnp.int32)


def draw_cos_zenith(key, part):
    key = jax.random.fold_in(key, 13)
    spread = jax.random.uniform(key, (COLS,), jnp.float32)
    values = 0.05 * jnp.exp(spread * jnp.log(20.0))
    return jnp.clip(values, 0.05, 1.0).astype(jnp.bfloat16)


def steps_of(key, shape, cuts, smallest, high):
    level = 1.0
    for position, blocks in cuts:
        steps = jax.random.uniform(jax.random.fold_in(jax.random.fold_in(key, 6), position), (blocks,), jnp.float32, smallest / len(cuts), high / len(cuts))
        level = level * jnp.repeat(jnp.exp(steps), shape[position] // blocks).reshape((-1,) + (1,) * (len(shape) - 1 - position))
    return level


def gaussian(own_key, dims, deviation, bound, cuts=(), kind=jnp.bfloat16):
    level = steps_of(own_key, dims, cuts, -0.22, 0.18) if cuts else 1.0
    result = jax.random.normal(own_key, dims, jnp.float32) * deviation * level
    return jnp.minimum(jnp.maximum(result, -bound), bound).astype(kind)


def setup_inputs(seed: int = 0) -> dict:
    key_list = jax.random.split(jax.random.key(seed), 13)
    return {
        "column_state": gaussian(key_list[0], (COLS, FEAT), 1.0, 6.0, ((0, 128),)),
        "sunlit": draw_sunlit(jax.random.fold_in(key_list[12], 71), 0),
        "flagged": draw_flagged(jax.random.fold_in(key_list[12], 71), 0),
        "cos_zenith": draw_cos_zenith(jax.random.fold_in(key_list[12], 71), 0),
        "surface_albedo": jnp.clip(0.29882812 + 0.5996094 * jax.random.uniform(key_list[4], (COLS,), jnp.float32) ** steps_of(key_list[4], (COLS,), ((0, 128),), -0.2, 0.2), 0.29882812, 0.8984375).astype(jnp.bfloat16),
        "first_weight": gaussian(key_list[5], (MEMBERS, FEAT, HID), FEAT ** -0.5, 0.25, ((0, 4),)),
        "first_bias": gaussian(key_list[6], (MEMBERS, HID), 0.5, 3.0, ((0, 4),)),
        "second_weight": gaussian(key_list[7], (MEMBERS, HID, OUTW), HID ** -0.5, 0.1875, ((0, 4),)),
        "second_bias": gaussian(key_list[8], (MEMBERS, OUTW), 0.5, 3.0, ((0, 4),)),
        "absorption": jnp.clip(jnp.exp(math.log(0.15625) - 6.9077553 * jax.random.uniform(key_list[9], (G, LEV), jnp.float32) ** steps_of(key_list[9], (G, LEV), ((0, 4),), -0.2, 0.2)), 0.00015625, 0.15625),
        "scatter_albedo": jnp.clip(0.85 + 0.14499998 * jax.random.uniform(key_list[10], (G,), jnp.float32) ** steps_of(key_list[10], (G,), ((0, 4),), -0.2, 0.2), 0.85, 0.995),
        "solar_weight": jnp.clip(jnp.exp(math.log(0.04464286) - 2.3025851 * jax.random.uniform(key_list[11], (G,), jnp.float32) ** steps_of(key_list[11], (G,), ((0, 4),), -0.2, 0.2)), 0.004464286, 0.04464286),
    }


diffusivity = 1.66


def member_flux(column_rows, weight_one, bias_one, weight_two, bias_two):
    pre_act = jnp.dot(column_rows, weight_one, preferred_element_type=jnp.float32) + bias_one.astype(jnp.float32)
    hidden = jax.nn.gelu(pre_act, approximate=False).astype(jnp.bfloat16)
    return jnp.dot(hidden, weight_two, preferred_element_type=jnp.float32) + bias_two.astype(jnp.float32)


def exclusive_prefix(values):
    running = jnp.cumsum(values, axis=2)
    return jnp.concatenate([jnp.zeros_like(values[..., :1]), running[..., :-1]], axis=2)


def inclusive_suffix(values):
    return jnp.flip(jnp.cumsum(jnp.flip(values, 2), axis=2), 2)


def two_stream(humidity, zenith, top_flux, albedo, absorption, scatter_albedo, solar_weight):
    optical = absorption[:, None, :] * humidity[None]
    depth_above = exclusive_prefix(optical)
    column_depth = depth_above[..., -1] + optical[..., -1]
    slant = 1.0 / zenith
    incident = solar_weight[:, None] * top_flux[None, :]
    omega = scatter_albedo[:, None, None]
    direct = incident[..., None] * jnp.exp(-depth_above * slant[None, :, None])
    first_source = 0.5 * omega * direct * (-jnp.expm1(-optical * slant[None, :, None]))
    ground_direct = incident * jnp.exp(-column_depth * slant[None, :])
    fall = jnp.exp(-diffusivity * depth_above)
    rise = jnp.exp(diffusivity * depth_above)
    rise_below = jnp.exp(diffusivity * (depth_above + optical))
    fall_ground = jnp.exp(-diffusivity * column_depth)
    lost = 0.5 * omega * (-jnp.expm1(-diffusivity * optical))

    def transport(source):
        climbing = source * rise_below
        down = fall * exclusive_prefix(climbing)
        ground_up = albedo[None, :] * (ground_direct + fall_ground * jnp.sum(climbing, axis=2))
        up = rise * (inclusive_suffix(fall * source) + (fall_ground * ground_up)[..., None])
        return down, up, ground_up

    source = first_source
    for sweep in range(SWEEPS):
        down, up, ground_up = transport(source)
        up_below = jnp.concatenate([up[..., 1:], ground_up[..., None]], axis=2)
        source = first_source + lost * (down + up_below)
    down, up, ground_up = transport(source)
    return jnp.sum(direct + down - up, axis=0)


def reference(column_state, sunlit, flagged, cos_zenith, surface_albedo, first_weight, first_bias, second_weight, second_bias, absorption, scatter_albedo, solar_weight):
    def one_block(block_rows):
        committee = jnp.zeros((block_rows.shape[0], 2 * LEV), jnp.float32)
        for member in range(MEMBERS):
            committee = committee + member_flux(block_rows, first_weight[member], first_bias[member], second_weight[member], second_bias[member]) / MEMBERS
        return committee

    committee = lax.map(one_block, column_state.reshape(N_TILE, COLS_T, FEAT)).reshape(COLS, OUTW)

    picked = jnp.nonzero(flagged == 1, size=COLS // 4)[0].astype(jnp.int32)
    moisture = column_state[picked, LEV:2 * LEV].reshape(N_TILE, PER, LEV)
    zenith_rows = cos_zenith[picked].astype(jnp.float32).reshape(N_TILE, PER)
    lit_rows = sunlit[picked].astype(jnp.float32).reshape(N_TILE, PER)
    albedo_rows = surface_albedo[picked].astype(jnp.float32).reshape(N_TILE, PER)

    def exact_block(pieces):
        block_moisture, block_zenith, block_lit, block_albedo = pieces
        humidity = 1.0 + 0.5 * jnp.tanh(block_moisture.astype(jnp.float32))
        return two_stream(humidity, block_zenith, block_zenith * block_lit, block_albedo, absorption, scatter_albedo, solar_weight)

    exact_rows = lax.map(exact_block, (moisture, zenith_rows, lit_rows, albedo_rows)).reshape(COLS // 4, LEV)
    exact_all = jnp.zeros((COLS, LEV), jnp.float32).at[picked].set(exact_rows)
    chosen = flagged.astype(jnp.float32)
    lit_mask = sunlit.astype(jnp.float32)
    short_wave = chosen[:, None] * exact_all + (1.0 - chosen[:, None]) * lit_mask[:, None] * committee[:, :LEV]
    return jnp.concatenate([short_wave, committee[:, LEV:]], axis=1)
```

```python
import math

import jax
import jax.numpy as jnp
from jax import lax
from jax.experimental import pallas as pl
from jax.experimental.pallas import tpu as pltpu
from jax.sharding import PartitionSpec as P

SWEEPS = 4
DIFFUSIVITY = 1.66
LOG2E = 1.0 / math.log(2.0)
SUBLANES = 8
UNROLL = 8


def gelu(values):
    return 0.5 * values * (1.0 + lax.erf(values * math.sqrt(0.5)))


def group_sum(values):
    rows, lanes = values.shape
    return jnp.sum(values.reshape(rows // SUBLANES, SUBLANES, lanes), axis=0)


def column_kernel(
    state_ref,
    sunlit_ref,
    flagged_ref,
    zenith_ref,
    albedo_ref,
    bias_one_ref,
    bias_two_ref,
    absorption_ref,
    scatter_ref,
    solar_ref,
    weight_one_hbm,
    weight_two_hbm,
    out_ref,
    weight_one,
    weight_two,
    humid,
    humid_slant,
    keep,
    lost,
    source,
    falling,
    total,
    weight_sems,
):
    copy_one = pltpu.make_async_copy(weight_one_hbm, weight_one, weight_sems.at[0])
    copy_two = pltpu.make_async_copy(weight_two_hbm, weight_two, weight_sems.at[1])
    copy_one.start()
    copy_two.start()

    groups, levels = absorption_ref.shape
    columns = state_ref.shape[0]

    lit = sunlit_ref[...].astype(jnp.float32)
    chosen = flagged_ref[...].astype(jnp.float32)
    zenith = zenith_ref[...].astype(jnp.float32)
    albedo = albedo_ref[...].astype(jnp.float32)

    moisture = state_ref[:, levels : 2 * levels].astype(jnp.float32)
    humidity = (1.0 + 0.5 * jnp.tanh(moisture)).T
    humid[...] = humidity
    humid_slant[...] = humidity * (1.0 / (DIFFUSIVITY * zenith))
    scaled = absorption_ref[...] * (-DIFFUSIVITY * LOG2E)

    half_omega = jnp.broadcast_to(0.5 * scatter_ref[...], (levels, groups)).T
    half_omega = jnp.broadcast_to(half_omega[:, :1], (groups, columns))
    solar = jnp.broadcast_to(solar_ref[...], (levels, groups)).T
    solar = jnp.broadcast_to(solar[:, :1], (groups, columns))

    def setup(block, carry):
        direct, down = carry
        first_level = block * UNROLL
        window = pltpu.roll(scaled, (levels - first_level) % levels, 1)
        for step in range(UNROLL):
            level = first_level + step
            extinction = jnp.broadcast_to(window[:, step : step + 1], (groups, columns))
            passed = jnp.exp2(extinction * humid[pl.ds(level, 1), :])
            beam = jnp.exp2(extinction * humid_slant[pl.ds(level, 1), :])
            below = direct * beam
            first = half_omega * (direct - below)
            keep[level] = passed
            lost[level] = half_omega - half_omega * passed
            source[level] = first
            falling[level] = down
            total[level] = group_sum(direct)
            down = passed * down + first
            direct = below
        return direct, down

    nothing = jnp.zeros((groups, columns), jnp.float32)
    direct, down = lax.fori_loop(
        0, levels // UNROLL, setup, (solar * (zenith * lit), nothing)
    )

    def descend(last):
        def body(block, up):
            for step in range(UNROLL):
                level = levels - 1 - (block * UNROLL + step)
                falls = falling[level]
                emitted = source[level]
                if not last:
                    source[level] = lost[level] * (falls + up)
                up = keep[level] * up + emitted
                total[level] += group_sum(falls - up)
            return up

        return body

    def ascend(block, down):
        for step in range(UNROLL):
            level = block * UNROLL + step
            falling[level] = down
            down = keep[level] * down + source[level]
        return down

    up = albedo * (direct + down)
    for sweep in range(SWEEPS):
        lax.fori_loop(0, levels // UNROLL, descend(False), up)
        down = lax.fori_loop(0, levels // UNROLL, ascend, nothing)
        up = albedo * down
    lax.fori_loop(0, levels // UNROLL, descend(True), up)

    exact = (jnp.sum(total[...], axis=1) * chosen).T

    copy_one.wait()
    hidden = jnp.dot(state_ref[...], weight_one[...], preferred_element_type=jnp.float32)
    hidden = gelu(hidden + bias_one_ref[...].astype(jnp.float32)).astype(jnp.bfloat16)
    copy_two.wait()
    guess = jnp.dot(hidden, weight_two[...], preferred_element_type=jnp.float32)
    guess = 0.25 * (guess + bias_two_ref[...].astype(jnp.float32))
    mask = jnp.broadcast_to((1.0 - chosen) * lit, (levels, columns)).T
    out_ref[:, :levels] = exact + mask * guess[:, :levels]
    out_ref[:, levels:] = guess[:, levels:]


def shards(
    column_state,
    sunlit,
    flagged,
    cos_zenith,
    surface_albedo,
    first_weight,
    first_bias,
    second_weight,
    second_bias,
    absorption,
    scatter_albedo,
    solar_weight,
):
    columns, features = column_state.shape
    groups, levels = absorption.shape
    hidden = first_weight.shape[2]
    outputs = second_weight.shape[2]
    bands = lax.axis_size("band")
    in_vmem = pl.BlockSpec(memory_space=pltpu.VMEM)
    in_place = pl.BlockSpec(memory_space=pl.ANY)
    by_level = pltpu.VMEM((levels, groups, columns), jnp.float32)
    terms = pl.pallas_call(
        column_kernel,
        out_shape=jax.ShapeDtypeStruct((columns, outputs), jnp.float32),
        in_specs=[in_vmem] * 10 + [in_place] * 2,
        out_specs=in_vmem,
        scratch_shapes=[
            pltpu.VMEM((features, hidden), jnp.bfloat16),
            pltpu.VMEM((hidden, outputs), jnp.bfloat16),
            pltpu.VMEM((levels, columns), jnp.float32),
            pltpu.VMEM((levels, columns), jnp.float32),
            by_level,
            by_level,
            by_level,
            by_level,
            pltpu.VMEM((levels, SUBLANES, columns), jnp.float32),
            pltpu.SemaphoreType.DMA((2,)),
        ],
        compiler_params=pltpu.CompilerParams(vmem_limit_bytes=48 * 1024 * 1024),
        name="column_terms",
    )(
        column_state,
        sunlit.reshape(1, columns),
        flagged.reshape(1, columns),
        cos_zenith.reshape(1, columns),
        surface_albedo.reshape(1, columns),
        first_bias,
        second_bias,
        absorption,
        scatter_albedo.reshape(1, groups),
        solar_weight.reshape(1, groups),
        first_weight[0],
        second_weight[0],
    )
    blocks = lax.all_to_all(
        terms.reshape(bands, columns // bands, outputs), "band", split_axis=0, concat_axis=0, tiled=True
    )
    return jnp.sum(blocks, axis=0)


def solution(mesh):
    in_specs = (
        P("tile", None),
        P("tile"),
        P("tile"),
        P("tile"),
        P("tile"),
        P("band", None, None),
        P("band", None),
        P("band", None, None),
        P("band", None),
        P("band", None),
        P("band"),
        P("band"),
    )
    out_specs = P(("tile", "band"), None)
    return jax.shard_map(shards, mesh=mesh, in_specs=in_specs, out_specs=out_specs, check_vma=False)
```

```python
import math

import jax
import jax.numpy as jnp
from jax import lax
from jax.experimental import pallas as pl
from jax.experimental.pallas import tpu as pltpu
from jax.sharding import PartitionSpec as P

SWEEPS = 4
DIFFUSIVITY = 1.66
LOG2E = 1.0 / math.log(2.0)
SUBLANES = 8
DESCENT = 32


def gelu(values):
    return 0.5 * values * (1.0 + lax.erf(values * math.sqrt(0.5)))


def group_sum(values):
    return jnp.sum(values, axis=0)


def column_kernel(*refs):
    hbm, out_ref, local, (humid, humid_slant, keep, lost, source, falling, total, sems) = (
        refs[:12],
        refs[12],
        refs[13:25],
        refs[25:],
    )
    copies = [pltpu.make_async_copy(a, b, sems.at[i]) for i, (a, b) in enumerate(zip(hbm, local))]
    for copy in copies:
        copy.start()
    (
        state_ref,
        sunlit_ref,
        flagged_ref,
        zenith_ref,
        albedo_ref,
        bias_one_ref,
        bias_two_ref,
        absorption_ref,
        scatter_ref,
        solar_ref,
        weight_one_ref,
        weight_two_ref,
    ) = local
    for copy in copies[:10]:
        copy.wait()

    groups, levels = absorption_ref.shape
    columns = state_ref.shape[0]

    chains = groups // SUBLANES
    wide = (chains, SUBLANES, columns)

    def rows(level):
        return pl.ds(level * chains, chains)

    lit = sunlit_ref[...].astype(jnp.float32)
    chosen = flagged_ref[...].astype(jnp.float32)
    zenith = zenith_ref[...].astype(jnp.float32)
    albedo = albedo_ref[...].astype(jnp.float32)

    moisture = state_ref[:, levels : 2 * levels].astype(jnp.float32)
    humidity = (1.0 + 0.5 * jnp.tanh(moisture)).T
    humid[...] = humidity
    humid_slant[...] = humidity * (1.0 / (DIFFUSIVITY * zenith))
    scaled = absorption_ref[...] * (-DIFFUSIVITY * LOG2E)

    half_omega = jnp.broadcast_to(0.5 * scatter_ref[...], (levels, groups)).T
    half_omega = jnp.broadcast_to(half_omega[:, :1], (groups, columns)).reshape(wide)
    solar = jnp.broadcast_to(solar_ref[...], (levels, groups)).T
    solar = jnp.broadcast_to(solar[:, :1], (groups, columns)).reshape(wide)

    nothing = jnp.zeros(wide, jnp.float32)
    direct = solar * (zenith * lit)
    down = nothing
    for level in range(levels):
        extinction = jnp.broadcast_to(scaled[:, level : level + 1], (groups, columns)).reshape(wide)
        passed = jnp.exp2(extinction * humid[pl.ds(level, 1), :])
        beam = jnp.exp2(extinction * humid_slant[pl.ds(level, 1), :])
        below = direct * beam
        first = half_omega * (direct - below)
        keep[rows(level)] = passed
        lost[rows(level)] = half_omega - half_omega * passed
        source[rows(level)] = first
        falling[rows(level)] = down
        total[level] = group_sum(direct)
        down = passed * down + first
        direct = below

    def descend(last):
        def body(block, up):
            for step in range(DESCENT):
                level = levels - 1 - (block * DESCENT + step)
                falls = falling[rows(level)]
                emitted = source[rows(level)]
                if not last:
                    source[rows(level)] = lost[rows(level)] * (falls + up)
                up = keep[rows(level)] * up + emitted
                total[level] += group_sum(falls - up)
            return up

        return body

    def ascend():
        down = nothing
        for level in range(levels):
            falling[rows(level)] = down
            down = keep[rows(level)] * down + source[rows(level)]
        return down

    up = albedo * (direct + down)
    for sweep in range(SWEEPS):
        lax.fori_loop(0, levels // DESCENT, descend(False), up)
        up = albedo * ascend()
    lax.fori_loop(0, levels // DESCENT, descend(True), up)

    exact = (jnp.sum(total[...], axis=1) * chosen).T

    copies[10].wait()
    hidden = jnp.dot(state_ref[...], weight_one_ref[...], preferred_element_type=jnp.float32)
    hidden = gelu(hidden + bias_one_ref[...].astype(jnp.float32)).astype(jnp.bfloat16)
    copies[11].wait()
    guess = jnp.dot(hidden, weight_two_ref[...], preferred_element_type=jnp.float32)
    guess = 0.25 * (guess + bias_two_ref[...].astype(jnp.float32))
    mask = jnp.broadcast_to((1.0 - chosen) * lit, (levels, columns)).T
    out_ref[:, :levels] = exact + mask * guess[:, :levels]
    out_ref[:, levels:] = guess[:, levels:]


def shards(
    column_state,
    sunlit,
    flagged,
    cos_zenith,
    surface_albedo,
    first_weight,
    first_bias,
    second_weight,
    second_bias,
    absorption,
    scatter_albedo,
    solar_weight,
):
    columns, features = column_state.shape
    groups, levels = absorption.shape
    hidden = first_weight.shape[2]
    outputs = second_weight.shape[2]
    bands = lax.axis_size("band")
    operands = (
        column_state,
        sunlit.reshape(1, columns),
        flagged.reshape(1, columns),
        cos_zenith.reshape(1, columns),
        surface_albedo.reshape(1, columns),
        first_bias,
        second_bias,
        absorption,
        scatter_albedo.reshape(1, groups),
        solar_weight.reshape(1, groups),
        first_weight[0],
        second_weight[0],
    )
    chain_rows = levels * groups // SUBLANES
    terms = pl.pallas_call(
        column_kernel,
        out_shape=jax.ShapeDtypeStruct((columns, outputs), jnp.float32),
        in_specs=[pl.BlockSpec(memory_space=pltpu.HBM)] * len(operands),
        out_specs=pl.BlockSpec(memory_space=pltpu.VMEM),
        scratch_shapes=[pltpu.VMEM(x.shape, x.dtype) for x in operands]
        + [pltpu.VMEM((levels, columns), jnp.float32)] * 2
        + [pltpu.VMEM((chain_rows, SUBLANES, columns), jnp.float32)] * 4
        + [pltpu.VMEM((levels, SUBLANES, columns), jnp.float32)]
        + [pltpu.SemaphoreType.DMA((len(operands),))],
        compiler_params=pltpu.CompilerParams(vmem_limit_bytes=48 * 1024 * 1024),
        name="column_terms",
    )(*[pltpu.with_memory_space_constraint(x, pltpu.HBM) for x in operands])
    blocks = lax.all_to_all(
        terms.reshape(bands, columns // bands, outputs), "band", split_axis=0, concat_axis=0, tiled=True
    )
    return jnp.sum(blocks, axis=0)


def solution(mesh):
    in_specs = (
        P("tile", None),
        P("tile"),
        P("tile"),
        P("tile"),
        P("tile"),
        P("band", None, None),
        P("band", None),
        P("band", None, None),
        P("band", None),
        P("band", None),
        P("band"),
        P("band"),
    )
    out_specs = P(("tile", "band"), None)
    return jax.shard_map(shards, mesh=mesh, in_specs=in_specs, out_specs=out_specs, check_vma=False)
```

```python
import math

import jax
import jax.numpy as jnp
from jax import lax
from jax.experimental import pallas as pl
from jax.experimental.pallas import tpu as pltpu
from jax.sharding import PartitionSpec as P

SWEEPS = 4
DIFFUSIVITY = 1.66
LOG2E = 1.0 / math.log(2.0)
SUBLANES = 8


def gelu(values):
    return 0.5 * values * (1.0 + lax.erf(values * math.sqrt(0.5)))


def group_sum(values):
    return jnp.sum(values, axis=0)


def column_kernel(*refs):
    hbm, out_ref, local, (humid, humid_slant, keep, lost, source, falling, total, sems) = (
        refs[:12],
        refs[12],
        refs[13:25],
        refs[25:],
    )
    copies = [pltpu.make_async_copy(a, b, sems.at[i]) for i, (a, b) in enumerate(zip(hbm, local))]
    for copy in copies[:10]:
        copy.start()
    (
        state_ref,
        sunlit_ref,
        flagged_ref,
        zenith_ref,
        albedo_ref,
        bias_one_ref,
        bias_two_ref,
        absorption_ref,
        scatter_ref,
        solar_ref,
        weight_one_ref,
        weight_two_ref,
    ) = local
    for copy in copies[:10]:
        copy.wait()
    for copy in copies[10:]:
        copy.start()

    groups, levels = absorption_ref.shape
    columns = state_ref.shape[0]

    chains = groups // SUBLANES
    wide = (chains, SUBLANES, columns)

    def rows(level):
        return pl.ds(level * chains, chains)

    lit = sunlit_ref[...].astype(jnp.float32)
    chosen = flagged_ref[...].astype(jnp.float32)
    zenith = zenith_ref[...].astype(jnp.float32)
    albedo = albedo_ref[...].astype(jnp.float32)

    moisture = state_ref[:, levels : 2 * levels].astype(jnp.float32)
    humidity = (1.0 + 0.5 * jnp.tanh(moisture)).T
    humid[...] = humidity
    humid_slant[...] = humidity * (1.0 / (DIFFUSIVITY * zenith))
    scaled = absorption_ref[...] * (-DIFFUSIVITY * LOG2E)

    half_omega = jnp.broadcast_to(0.5 * scatter_ref[...], (levels, groups)).T
    half_omega = jnp.broadcast_to(half_omega[:, :1], (groups, columns)).reshape(wide)
    solar = jnp.broadcast_to(solar_ref[...], (levels, groups)).T
    solar = jnp.broadcast_to(solar[:, :1], (groups, columns)).reshape(wide)

    nothing = jnp.zeros(wide, jnp.float32)
    direct = solar * (zenith * lit)
    down = nothing
    for level in range(levels):
        extinction = jnp.broadcast_to(scaled[:, level : level + 1], (groups, columns)).reshape(wide)
        passed = jnp.exp2(extinction * humid[pl.ds(level, 1), :])
        beam = jnp.exp2(extinction * humid_slant[pl.ds(level, 1), :])
        below = direct * beam
        first = half_omega * (direct - below)
        keep[rows(level)] = passed
        lost[rows(level)] = half_omega - half_omega * passed
        source[rows(level)] = first
        falling[rows(level)] = down
        total[level] = group_sum(direct)
        down = passed * down + first
        direct = below

    def descend(up, last):
        for level in reversed(range(levels)):
            falls = falling[rows(level)]
            emitted = source[rows(level)]
            if not last:
                source[rows(level)] = lost[rows(level)] * (falls + up)
            up = keep[rows(level)] * up + emitted
            net = total[level] + group_sum(falls - up)
            if last:
                humid[pl.ds(level, 1), :] = jnp.sum(net, axis=0, keepdims=True)
            else:
                total[level] = net

    def ascend():
        down = nothing
        for level in range(levels):
            falling[rows(level)] = down
            down = keep[rows(level)] * down + source[rows(level)]
        return down

    def sweep(_, up):
        descend(up, False)
        return albedo * ascend()

    up = lax.fori_loop(0, SWEEPS, sweep, albedo * (direct + down))
    for copy in copies[10:]:
        copy.wait()
    descend(up, True)

    exact = (humid[...] * chosen).T

    hidden = jnp.dot(state_ref[...], weight_one_ref[...], preferred_element_type=jnp.float32)
    hidden = gelu(hidden + bias_one_ref[...].astype(jnp.float32)).astype(jnp.bfloat16)
    guess = jnp.dot(hidden, weight_two_ref[...], preferred_element_type=jnp.float32)
    guess = 0.25 * (guess + bias_two_ref[...].astype(jnp.float32))
    mask = jnp.broadcast_to((1.0 - chosen) * lit, (levels, columns)).T
    out_ref[:, :levels] = exact + mask * guess[:, :levels]
    out_ref[:, levels:] = guess[:, levels:]


def shards(
    column_state,
    sunlit,
    flagged,
    cos_zenith,
    surface_albedo,
    first_weight,
    first_bias,
    second_weight,
    second_bias,
    absorption,
    scatter_albedo,
    solar_weight,
):
    columns, features = column_state.shape
    groups, levels = absorption.shape
    hidden = first_weight.shape[2]
    outputs = second_weight.shape[2]
    bands = lax.axis_size("band")
    operands = (
        column_state,
        sunlit.reshape(1, columns),
        flagged.reshape(1, columns),
        cos_zenith.reshape(1, columns),
        surface_albedo.reshape(1, columns),
        first_bias,
        second_bias,
        absorption,
        scatter_albedo.reshape(1, groups),
        solar_weight.reshape(1, groups),
        first_weight[0],
        second_weight[0],
    )
    chain_rows = levels * groups // SUBLANES
    terms = pl.pallas_call(
        column_kernel,
        out_shape=jax.ShapeDtypeStruct((columns, outputs), jnp.float32),
        in_specs=[pl.BlockSpec(memory_space=pltpu.HBM)] * len(operands),
        out_specs=pl.BlockSpec(memory_space=pltpu.VMEM),
        scratch_shapes=[pltpu.VMEM(x.shape, x.dtype) for x in operands]
        + [pltpu.VMEM((levels, columns), jnp.float32)] * 2
        + [pltpu.VMEM((chain_rows, SUBLANES, columns), jnp.float32)] * 4
        + [pltpu.VMEM((levels, SUBLANES, columns), jnp.float32)]
        + [pltpu.SemaphoreType.DMA((len(operands),))],
        compiler_params=pltpu.CompilerParams(vmem_limit_bytes=48 * 1024 * 1024),
        name="column_terms",
    )(*[pltpu.with_memory_space_constraint(x, pltpu.HBM) for x in operands])
    blocks = lax.all_to_all(
        terms.reshape(bands, columns // bands, outputs), "band", split_axis=0, concat_axis=0, tiled=True
    )
    return jnp.sum(blocks, axis=0)


def solution(mesh):
    in_specs = (
        P("tile", None),
        P("tile"),
        P("tile"),
        P("tile"),
        P("tile"),
        P("band", None, None),
        P("band", None),
        P("band", None, None),
        P("band", None),
        P("band", None),
        P("band"),
        P("band"),
    )
    out_specs = P(("tile", "band"), None)
    return jax.shard_map(shards, mesh=mesh, in_specs=in_specs, out_specs=out_specs, check_vma=False)
```

```python
import math

import jax
import jax.numpy as jnp
from jax import lax
from jax.experimental import pallas as pl
from jax.experimental.pallas import tpu as pltpu
from jax.sharding import PartitionSpec as P

SWEEPS = 4
DIFFUSIVITY = 1.66
LOG2E = 1.0 / math.log(2.0)
SUBLANES = 8
SHIFTED = 3


def twice_gelu(values):
    return values * (1.0 + lax.erf(values * math.sqrt(0.5)))


def group_sum(values):
    return jnp.sum(values, axis=0)


def column_kernel(*refs):
    hbm, out_ref, local, (humid, humid_slant, keep, lost, source, falling, total, sems) = (
        refs[:12],
        refs[12],
        refs[13:25],
        refs[25:],
    )
    copies = [pltpu.make_async_copy(a, b, sems.at[i]) for i, (a, b) in enumerate(zip(hbm, local))]
    for copy in copies[:7]:
        copy.start()
    (
        absorption_ref,
        state_ref,
        zenith_ref,
        scatter_ref,
        solar_ref,
        sunlit_ref,
        albedo_ref,
        flagged_ref,
        bias_one_ref,
        bias_two_ref,
        weight_one_ref,
        weight_two_ref,
    ) = local
    for copy in copies[7:]:
        copy.start()
    for copy in copies[:7]:
        copy.wait()

    groups, levels = absorption_ref.shape
    columns = state_ref.shape[0]

    chains = groups // SUBLANES
    wide = (chains, SUBLANES, columns)

    def rows(level):
        return pl.ds(level * chains, chains)

    lit = sunlit_ref[...].astype(jnp.float32)
    zenith = zenith_ref[...].astype(jnp.float32)
    albedo = albedo_ref[...].astype(jnp.float32)

    moisture = state_ref[:, levels : 2 * levels].astype(jnp.float32)
    humidity = (1.0 + 0.5 * jnp.tanh(moisture)).T
    humid[...] = humidity
    humid_slant[...] = humidity * (1.0 / (DIFFUSIVITY * zenith))
    scaled = absorption_ref[...] * (-DIFFUSIVITY * LOG2E)

    first_row = lax.broadcasted_iota(jnp.int32, (SUBLANES, groups), 0) == 0
    sides = jnp.where(first_row, 0.5 * scatter_ref[...], solar_ref[...]).T
    half_omega = jnp.broadcast_to(sides[:, :1], (groups, columns)).reshape(wide)
    solar = jnp.broadcast_to(sides[:, 1:2], (groups, columns)).reshape(wide)

    nothing = jnp.zeros(wide, jnp.float32)
    direct = solar * (zenith * lit)
    down = nothing
    for level in range(levels):
        extinction = jnp.broadcast_to(scaled[:, level : level + 1], (groups, columns)).reshape(wide)
        passed = jnp.exp2(extinction * humid[pl.ds(level, 1), :])
        beam = jnp.exp2(extinction * humid_slant[pl.ds(level, 1), :])
        below = direct * beam
        first = half_omega * (direct - below)
        keep[rows(level)] = passed
        lost[rows(level)] = half_omega - half_omega * passed
        source[rows(level)] = first
        falling[rows(level)] = down
        total[level] = group_sum(direct) + group_sum(down[:SHIFTED])
        down = passed * down + first
        direct = below

    def descend(up, last):
        for level in reversed(range(levels)):
            falls = falling[rows(level)]
            emitted = source[rows(level)]
            if not last:
                source[rows(level)] = lost[rows(level)] * (falls + up)
            up = keep[rows(level)] * up + emitted
            net = total[level] + group_sum(falls[SHIFTED:] - up[SHIFTED:]) - group_sum(up[:SHIFTED])
            if last:
                humid[pl.ds(level, 1), :] = jnp.sum(net, axis=0, keepdims=True)
            else:
                total[level] = net

    def ascend():
        down = nothing
        for level in range(levels):
            falling[rows(level)] = down
            total[level] += group_sum(down[:SHIFTED])
            down = keep[rows(level)] * down + source[rows(level)]
        return down

    def sweep(_, up):
        descend(up, False)
        return albedo * ascend()

    up = lax.fori_loop(0, SWEEPS, sweep, albedo * (direct + down))
    for copy in copies[7:]:
        copy.wait()
    descend(up, True)

    chosen = flagged_ref[...].astype(jnp.float32)
    exact = (humid[...] * chosen).T

    hidden = jnp.dot(state_ref[...], weight_one_ref[...], preferred_element_type=jnp.float32)
    hidden = twice_gelu(hidden + bias_one_ref[...].astype(jnp.float32)).astype(jnp.bfloat16)
    guess = jnp.dot(hidden, weight_two_ref[...], preferred_element_type=jnp.float32)
    guess = 0.125 * guess + 0.25 * bias_two_ref[...].astype(jnp.float32)
    mask = jnp.broadcast_to((1.0 - chosen) * lit, (levels, columns)).T
    out_ref[:, :levels] = exact + mask * guess[:, :levels]
    out_ref[:, levels:] = guess[:, levels:]


def shards(
    column_state,
    sunlit,
    flagged,
    cos_zenith,
    surface_albedo,
    first_weight,
    first_bias,
    second_weight,
    second_bias,
    absorption,
    scatter_albedo,
    solar_weight,
):
    columns, features = column_state.shape
    groups, levels = absorption.shape
    hidden = first_weight.shape[2]
    outputs = second_weight.shape[2]
    bands = lax.axis_size("band")
    operands = (
        absorption,
        column_state,
        cos_zenith.reshape(1, columns),
        scatter_albedo.reshape(1, groups),
        solar_weight.reshape(1, groups),
        sunlit.reshape(1, columns),
        surface_albedo.reshape(1, columns),
        flagged.reshape(1, columns),
        first_bias,
        second_bias,
        first_weight[0],
        second_weight[0],
    )
    chain_rows = levels * groups // SUBLANES
    terms = pl.pallas_call(
        column_kernel,
        out_shape=jax.ShapeDtypeStruct((columns, outputs), jnp.float32),
        in_specs=[pl.BlockSpec(memory_space=pltpu.HBM)] * len(operands),
        out_specs=pl.BlockSpec(memory_space=pltpu.VMEM),
        scratch_shapes=[pltpu.VMEM(x.shape, x.dtype) for x in operands]
        + [pltpu.VMEM((levels, columns), jnp.float32)] * 2
        + [pltpu.VMEM((chain_rows + SUBLANES, SUBLANES, columns), jnp.float32)] * 4
        + [pltpu.VMEM((levels, SUBLANES, columns), jnp.float32)]
        + [pltpu.SemaphoreType.DMA((len(operands),))],
        compiler_params=pltpu.CompilerParams(vmem_limit_bytes=48 * 1024 * 1024),
        name="column_terms",
    )(*[pltpu.with_memory_space_constraint(x, pltpu.HBM) for x in operands])
    blocks = lax.all_to_all(
        terms.reshape(bands, columns // bands, outputs), "band", split_axis=0, concat_axis=0, tiled=True
    )
    return jnp.sum(blocks, axis=0)


def solution(mesh):
    in_specs = (
        P("tile", None),
        P("tile"),
        P("tile"),
        P("tile"),
        P("tile"),
        P("band", None, None),
        P("band", None),
        P("band", None, None),
        P("band", None),
        P("band", None),
        P("band"),
        P("band"),
    )
    out_specs = P(("tile", "band"), None)
    return jax.shard_map(shards, mesh=mesh, in_specs=in_specs, out_specs=out_specs, check_vma=False)
```
